32 devices in a mesh: seq: 8 (over z, x), head: 4 (over y, core).
Axes of the slice: x: 2, y: 2, z: 4, core: 2. Of those that a mesh axis runs over, the one named last changes fastest.
Arguments:
- queries: bfloat16 [8192, 4096], P(('seq', 'head')), may hold values from -8 to 8
- key_rows: bfloat16 [8192, 2048], P(('seq', 'head')), may hold values from -8 to 8
- value_rows: bfloat16 [8192, 2048], P(('seq', 'head')), may hold values from -6 to 6
Outputs:
- attended: bfloat16 [8192, 4096], P(('seq', 'head'))
The draws below stay inside these ranges and needn't reach their ends.
All inputs are finite; a program needn't handle non-finite values.
Results may differ from the reference program's by a relative error of at most 0.0036.
Values may be sent and summed in bfloat16 or wider, within the bound.
A program may use at most 128 MiB of HBM per device.

```python
import jax
import jax.numpy as jnp
from jax import lax

HQ = 32
KV = 16
HD = 128
WINDOW = 1024
TOK_DEV = 256
SEQLEN = 8192
N_HEAD = 4


def base_rows(key, width):
    return jnp.clip(1.5 * jax.random.normal(jax.random.fold_in(key, 23), (SEQLEN, width), jnp.float32), -8.0, 8.0)


def draw_queries(key, part):
    base = base_rows(jax.random.fold_in(key, 1), HQ * HD)
    return base.astype(jnp.bfloat16)


def draw_key_rows(key, part):
    base = base_rows(jax.random.fold_in(key, 2), KV * HD)
    return base.astype(jnp.bfloat16)


def steps_of(rng, dims, cuts, low, top_value):
    def one(position, shards_of):
        steps = jax.random.uniform(jax.random.fold_in(jax.random.fold_in(rng, 6), position), (shards_of,), jnp.float32, low / len(cuts), top_value / len(cuts))
        return jnp.repeat(jnp.exp(steps), dims[position] // shards_of).reshape((-1,) + (1,) * (len(dims) - position - 1))

    level = one(*cuts[0])
    for cut in cuts[1:]:
        level = level * one(*cut)
    return level


def bell_draw(stream_key, extent, spread, limit, split=(), kind=jnp.bfloat16):
    entries = spread * jax.random.normal(stream_key, extent, jnp.float32)
    if split:
        entries = entries * steps_of(stream_key, extent, split, -0.22, 0.18)
    return jnp.clip(entries, -limit, limit).astype(kind)


def setup_inputs(seed: int = 0) -> dict:
    streams_of = jax.random.split(jax.random.key(seed), 4)
    queries = draw_queries(jax.random.fold_in(streams_of[3], 71), 0)
    key_rows = draw_key_rows(jax.random.fold_in(streams_of[3], 71), 0)
    value_rows = bell_draw(streams_of[2], (SEQLEN, KV * HD), 1.0, 6.0, ((0, 32),))
    return dict(queries=queries, key_rows=key_rows, value_rows=value_rows)


score_scale = 168.0 ** -0.5
neg_fill = -1e30


def reference(queries, key_rows, value_rows):
    block = TOK_DEV * N_HEAD
    rows = min(512, block)
    group = HQ // KV
    front = jnp.zeros((WINDOW, KV * HD), jnp.bfloat16)
    padded_keys = jnp.concatenate([front, key_rows], axis=0)
    padded_values = jnp.concatenate([front, value_rows], axis=0)

    def one_block(index_block):
        start = (index_block * rows).astype(jnp.int32)
        query_tile = lax.dynamic_slice_in_dim(queries, start, rows, 0).astype(jnp.float32).reshape(rows, KV, group, HD)
        key_tile = lax.dynamic_slice_in_dim(padded_keys, start, rows + WINDOW, 0).astype(jnp.float32).reshape(rows + WINDOW, KV, HD)
        value_tile = lax.dynamic_slice_in_dim(padded_values, start, rows + WINDOW, 0).astype(jnp.float32).reshape(rows + WINDOW, KV, HD)
        scores = jnp.einsum("qgrd,kgd->grqk", query_tile, key_tile) * score_scale
        query_pos = start + jnp.arange(rows, dtype=jnp.int32)
        key_pos = start - WINDOW + jnp.arange(rows + WINDOW, dtype=jnp.int32)
        spacing = query_pos[:, None] - key_pos[None, :]
        allowed = (spacing >= 0) & (spacing < WINDOW) & (key_pos[None, :] >= 0)
        scores = jnp.where(allowed, scores, jnp.float32(neg_fill))
        peak = jnp.max(scores, axis=-1, keepdims=True)
        expo = jnp.exp(scores - peak)
        total = jnp.sum(expo, axis=-1)
        weights = lax.optimization_barrier(expo.astype(jnp.bfloat16)).astype(jnp.float32)
        mixed = jnp.einsum("grqk,kgd->qgrd", weights, value_tile)
        mixed = mixed / jnp.transpose(total, (2, 0, 1))[..., None]
        return mixed.reshape(rows, HQ * HD).astype(jnp.bfloat16)

    result = lax.map(one_block, jnp.arange(SEQLEN // rows, dtype=jnp.int32))
    return result.reshape(SEQLEN, HQ * HD)
```

```python
import functools
import math

import jax
import jax.numpy as jnp
from jax import lax
from jax.experimental import pallas as pl
from jax.experimental.pallas import tpu as pltpu
from jax.sharding import PartitionSpec as P

HQ = 32
KV = 16
HD = 128
WINDOW = 1024
GROUP = HQ // KV
CHUNKS = 8

MESH = pl.DeviceIdType.MESH
exponent_scale = 168.0 ** (-0.5) * math.log2(math.e)
neg_fill = -1e30


def kernel(
    count,
    n_head,
    q_hbm,
    k_hbm,
    v_hbm,
    out_hbm,
    q_buf,
    k_buf,
    v_buf,
    out_buf,
    q_sem,
    own_sem,
    out_sem,
    send_sem,
    recv_sem,
):
    rows = q_hbm.shape[0]
    back = WINDOW // rows
    heads = KV // CHUNKS
    width = heads * HD
    me = lax.axis_index("seq") * n_head + lax.axis_index("head")
    core = lax.rem(me, 2)
    odd_chip = lax.rem(me // 2, 2)
    sibling = me + 1 - 2 * core
    across = me + 2 - 4 * odd_chip
    has_next = me + back < count
    has_far = me >= back
    has_mid = me >= 2

    def place(rank):
        return (rank // n_head, lax.rem(rank, n_head))

    def columns(g):
        return pl.ds(pl.multiple_of(g * width, width), width)

    def slot(distance):
        return pl.ds((back - distance) * rows, rows)

    own = (k_hbm, v_hbm)
    held = (k_buf, v_buf)

    def send(kind, g, which, source, distance, target):
        if source == 0:
            src = own[which].at[:, columns(g)]
        else:
            src = held[which].at[slot(source), columns(g)]
        return pltpu.make_async_remote_copy(
            src_ref=src,
            dst_ref=held[which].at[slot(distance), columns(g)],
            send_sem=send_sem.at[kind, g, which],
            recv_sem=recv_sem.at[distance - 1, g, which],
            device_id=place(target),
            device_id_type=MESH,
        )

    def sends(g):
        return {
            "next": (has_next, 0, 0, back, me + back),
            "core": (core == 0, 1, 0, 1, sibling),
            "up": (odd_chip == 0, 2, 0, 2, across),
            "down": ((odd_chip == 1) & has_far, 2, back, 2, across),
            "far": ((core == 1) & has_far, 3, back, 3, sibling),
            "mid0": ((core == 0) & has_mid, 4, 2, 3, sibling),
            "mid1": ((core == 1) & has_mid, 4, 2, 1, sibling),
        }

    def start(g, *names):
        for name in names:
            condition, kind, source, distance, target = sends(g)[name]

            @pl.when(condition)
            def _():
                for which in range(2):
                    send(kind, g, which, source, distance, target).start()

    def arrived(g, distance):
        for which in range(2):
            send(0, g, which, distance, distance, sibling).wait_recv()

    def load_own(g, which):
        return pltpu.make_async_copy(
            own[which].at[:, columns(g)], held[which].at[slot(0), columns(g)], own_sem.at[g, which]
        )

    def q_columns(g):
        return pl.ds(pl.multiple_of(g * width * GROUP, width * GROUP), width * GROUP)

    def load_q(g):
        return pltpu.make_async_copy(q_hbm.at[:, q_columns(g)], q_buf.at[:, q_columns(g)], q_sem.at[g])

    def store_out(g):
        return pltpu.make_async_copy(
            out_buf.at[:, q_columns(g)], out_hbm.at[:, q_columns(g)], out_sem.at[g]
        )

    def attend(g, checked):
        row = lax.broadcasted_iota(jnp.int32, (rows, rows), 0)
        column = lax.broadcasted_iota(jnp.int32, (rows, rows), 1)
        for local in range(heads):
            head = g * heads + local
            at = pl.ds(pl.multiple_of(head * HD, HD), HD)
            keys = k_buf[:, at]
            values = v_buf[:, at]
            for r in range(GROUP):
                q_at = pl.ds(pl.multiple_of((head * GROUP + r) * HD, HD), HD)
                scores = lax.dot_general(
                    q_buf[:, q_at], keys, (((1,), (1,)), ((), ())), preferred_element_type=jnp.float32
                )
                pieces = []
                for j in range(back + 1):
                    piece = scores[:, j * rows : (j + 1) * rows]
                    keep = None
                    if j == 0:
                        keep = column > row
                    elif j == back:
                        keep = column <= row
                    if checked and j < back:
                        there = jnp.full((rows, rows), me - back + j, jnp.int32) >= 0
                        keep = there if keep is None else keep & there
                    pieces.append(piece if keep is None else jnp.where(keep, piece, neg_fill))
                scores = jnp.concatenate(pieces, axis=1)
                peak = jnp.max(scores, axis=1, keepdims=True)
                expo = jnp.exp2((scores - peak) * exponent_scale)
                total = jnp.sum(expo, axis=1, keepdims=True)
                mixed = jnp.dot(expo.astype(jnp.bfloat16), values, preferred_element_type=jnp.float32)
                out_buf[:, q_at] = (mixed / total).astype(jnp.bfloat16)

    barrier = pltpu.get_barrier_semaphore()
    for target in (sibling, across):
        pl.semaphore_signal(barrier, inc=1, device_id=place(target), device_id_type=MESH)

    @pl.when(has_next)
    def _():
        pl.semaphore_signal(barrier, inc=1, device_id=place(me + back), device_id_type=MESH)

    @pl.when(has_far)
    def _():
        pl.semaphore_signal(barrier, inc=1, device_id=place(me - back), device_id_type=MESH)

    for distance in range(1, back + 1):

        @pl.when(me < distance)
        def _():
            for which in range(2):
                held[which][slot(distance), :] = jnp.zeros((rows, KV * HD), jnp.bfloat16)

    pl.semaphore_wait(barrier, 2 + has_next.astype(jnp.int32) + has_far.astype(jnp.int32))

    @pl.loop(0, CHUNKS)
    def _(g):
        start(g, "next", "up", "core")

    @pl.loop(0, CHUNKS)
    def _(g):
        load_q(g).start()
        for which in range(2):
            load_own(g, which).start()

    @pl.loop(0, CHUNKS + 2)
    def _(t):
        @pl.when((t < CHUNKS) & has_far)
        def _():
            arrived(t, back)
            start(t, "down", "far")

        mid = t - 1

        @pl.when((mid >= 0) & (mid < CHUNKS) & has_mid)
        def _():
            arrived(mid, 2)
            start(mid, "mid0", "mid1")

        g = t - 2

        @pl.when(g >= 0)
        def _():
            @pl.when(me >= 1)
            def _():
                arrived(g, 1)

            @pl.when(me >= 3)
            def _():
                arrived(g, 3)

            load_q(g).wait()
            for which in range(2):
                load_own(g, which).wait()

            @pl.when(has_far)
            def _():
                attend(g, False)

            @pl.when(me < back)
            def _():
                attend(g, True)

            store_out(g).start()

    @pl.loop(0, CHUNKS)
    def _(g):
        store_out(g).wait()
        for condition, kind, source, distance, target in sends(g).values():

            @pl.when(condition)
            def _():
                for which in range(2):
                    send(kind, g, which, source, distance, target).wait_send()


def solution(mesh):
    n_head = mesh.shape["head"]
    count = mesh.shape["seq"] * n_head

    def on_device(queries, key_rows, value_rows):
        rows = queries.shape[0]
        assert rows * 4 == WINDOW and n_head % 4 == 0
        span = rows + WINDOW
        return pl.pallas_call(
            functools.partial(kernel, count, n_head),
            out_shape=jax.ShapeDtypeStruct(queries.shape, queries.dtype),
            in_specs=[pl.BlockSpec(memory_space=pl.ANY)] * 3,
            out_specs=pl.BlockSpec(memory_space=pl.ANY),
            scratch_shapes=[
                pltpu.VMEM(queries.shape, jnp.bfloat16),
                pltpu.VMEM((span, KV * HD), jnp.bfloat16),
                pltpu.VMEM((span, KV * HD), jnp.bfloat16),
                pltpu.VMEM(queries.shape, jnp.bfloat16),
                pltpu.SemaphoreType.DMA((CHUNKS,)),
                pltpu.SemaphoreType.DMA((CHUNKS, 2)),
                pltpu.SemaphoreType.DMA((CHUNKS,)),
                pltpu.SemaphoreType.DMA((5, CHUNKS, 2)),
                pltpu.SemaphoreType.DMA((4, CHUNKS, 2)),
            ],
            compiler_params=pltpu.CompilerParams(
                collective_id=0, has_side_effects=True, vmem_limit_bytes=60 * 1024 * 1024
            ),
            cost_estimate=pl.CostEstimate(
                flops=4 * HQ * rows * span * HD,
                bytes_accessed=16 * 1024 * 1024,
                transcendentals=HQ * rows * span,
            ),
        )(queries, key_rows, value_rows)

    placed = P(("seq", "head"), None)
    return jax.shard_map(
        on_device, mesh=mesh, in_specs=(placed, placed, placed), out_specs=placed, check_vma=False
    )
```

```python
import functools
import math

import jax
import jax.numpy as jnp
from jax import lax
from jax.experimental import pallas as pl
from jax.experimental.pallas import tpu as pltpu
from jax.sharding import PartitionSpec as P

HQ = 32
KV = 16
HD = 128
WINDOW = 1024
GROUP = HQ // KV
CHUNKS = 16
AHEAD = 4

MESH = pl.DeviceIdType.MESH
exponent_scale = 168.0 ** (-0.5) * math.log2(math.e)
neg_fill = -1e30


def kernel(
    count,
    n_head,
    q_hbm,
    k_hbm,
    v_hbm,
    out_hbm,
    q_buf,
    k_buf,
    v_buf,
    out_buf,
    q_sem,
    own_sem,
    out_sem,
    core_sem,
    send_sem,
    recv_sem,
):
    rows = q_hbm.shape[0]
    back = WINDOW // rows
    heads = KV // CHUNKS
    width = heads * HD
    me = lax.axis_index("seq") * n_head + lax.axis_index("head")
    core = lax.rem(me, 2)
    odd_chip = lax.rem(me // 2, 2)
    sibling = me + 1 - 2 * core
    across = me + 2 - 4 * odd_chip
    has_next = me + back < count
    has_far = me >= back
    has_mid = me >= 2

    def place(rank):
        return (rank // n_head, lax.rem(rank, n_head))

    def columns(g):
        return pl.ds(pl.multiple_of(g * width, width), width)

    def slot(distance):
        return pl.ds((back - distance) * rows, rows)

    own = (k_hbm, v_hbm)
    held = (k_buf, v_buf)

    def send(kind, g, which, source, distance, target):
        if source == 0:
            src = own[which].at[:, columns(g)]
        else:
            src = held[which].at[slot(source), columns(g)]
        return pltpu.make_async_remote_copy(
            src_ref=src,
            dst_ref=held[which].at[slot(distance), columns(g)],
            send_sem=send_sem.at[kind, which],
            recv_sem=recv_sem.at[distance - 1, g, which],
            device_id=place(target),
            device_id_type=MESH,
        )

    def sends(g):
        return {
            "next": (has_next, 0, 0, back, me + back),
            "up": (odd_chip == 0, 1, 0, 2, across),
            "down": ((odd_chip == 1) & has_far, 1, back, 2, across),
            "far": ((core == 1) & has_far, 2, back, 3, sibling),
            "mid0": ((core == 0) & has_mid, 3, 2, 3, sibling),
            "mid1": ((core == 1) & has_mid, 3, 2, 1, sibling),
        }

    def start(g, which, *names):
        for name in names:
            condition, kind, source, distance, target = sends(g)[name]

            @pl.when(condition)
            def _():
                send(kind, g, which, source, distance, target).start()

    def arrived(g, which, distance):
        send(0, g, which, distance, distance, sibling).wait_recv()

    def load_own(which):
        return pltpu.make_async_copy(own[which], held[which].at[slot(0), :], own_sem.at[which])

    def send_core(which):
        return pltpu.make_async_remote_copy(
            src_ref=own[which],
            dst_ref=held[which].at[slot(1), :],
            send_sem=core_sem.at[0, which],
            recv_sem=core_sem.at[1, which],
            device_id=place(sibling),
            device_id_type=MESH,
        )

    def q_columns(g):
        return pl.ds(pl.multiple_of(g * width * GROUP, width * GROUP), width * GROUP)

    def load_q():
        return pltpu.make_async_copy(q_hbm, q_buf, q_sem)

    def store_out(g):
        return pltpu.make_async_copy(
            out_buf.at[:, q_columns(g)], out_hbm.at[:, q_columns(g)], out_sem
        )

    def attend(g, checked):
        row = lax.broadcasted_iota(jnp.int32, (rows, rows), 0)
        column = lax.broadcasted_iota(jnp.int32, (rows, rows), 1)
        for local in range(heads):
            head = g * heads + local
            at = pl.ds(pl.multiple_of(head * HD, HD), HD)
            keys = k_buf[:, at]
            values = v_buf[:, at]
            for r in range(GROUP):
                q_at = pl.ds(pl.multiple_of((head * GROUP + r) * HD, HD), HD)
                scores = lax.dot_general(
                    q_buf[:, q_at], keys, (((1,), (1,)), ((), ())), preferred_element_type=jnp.float32
                )
                pieces = []
                for j in range(back + 1):
                    piece = scores[:, j * rows : (j + 1) * rows]
                    keep = None
                    if j == 0:
                        keep = column > row
                    elif j == back:
                        keep = column <= row
                    if checked and j < back:
                        there = jnp.full((rows, rows), me - back + j, jnp.int32) >= 0
                        keep = there if keep is None else keep & there
                    pieces.append(piece if keep is None else jnp.where(keep, piece, neg_fill))
                scores = jnp.concatenate(pieces, axis=1)
                peak = jnp.max(scores, axis=1, keepdims=True)
                expo = jnp.exp2((scores - peak) * exponent_scale)
                total = jnp.sum(expo, axis=1, keepdims=True)
                mixed = jnp.dot(expo.astype(jnp.bfloat16), values, preferred_element_type=jnp.float32)
                out_buf[:, q_at] = (mixed / total).astype(jnp.bfloat16)

    barrier = pltpu.get_barrier_semaphore()
    for target in (sibling, across):
        pl.semaphore_signal(barrier, inc=1, device_id=place(target), device_id_type=MESH)

    @pl.when(has_next)
    def _():
        pl.semaphore_signal(barrier, inc=1, device_id=place(me + back), device_id_type=MESH)

    @pl.when(has_far)
    def _():
        pl.semaphore_signal(barrier, inc=1, device_id=place(me - back), device_id_type=MESH)

    pl.semaphore_wait(barrier, 2 + has_next.astype(jnp.int32) + has_far.astype(jnp.int32))

    def start_own(g):
        for which in range(2):
            start(g, which, "next", "up")

    for g in range(AHEAD):
        start_own(g)

    @pl.when(core == 0)
    def _():
        for which in range(2):
            send_core(which).start()

    load_q().start()
    for which in range(2):
        load_own(which).start()

    for distance in range(1, back + 1):

        @pl.when(me < distance)
        def _():
            for which in range(2):
                held[which][slot(distance), :] = jnp.zeros((rows, KV * HD), jnp.bfloat16)

    @pl.loop(0, CHUNKS + 2)
    def _(t):
        @pl.when(t + AHEAD < CHUNKS)
        def _():
            start_own(t + AHEAD)

        @pl.when((t < CHUNKS) & has_far)
        def _():
            for which in range(2):
                arrived(t, which, back)
                start(t, which, "down", "far")

        mid = t - 1

        @pl.when((mid >= 0) & (mid < CHUNKS) & has_mid)
        def _():
            for which in range(2):
                arrived(mid, which, 2)
                start(mid, which, "mid0", "mid1")

        g = t - 2

        @pl.when(g >= 0)
        def _():
            @pl.when((core == 0) & (me >= 1))
            def _():
                for which in range(2):
                    arrived(g, which, 1)

            @pl.when((core == 1) & (g == 0))
            def _():
                for which in range(2):
                    send_core(which).wait_recv()

            @pl.when(me >= 3)
            def _():
                for which in range(2):
                    arrived(g, which, 3)

            @pl.when(g == 0)
            def _():
                load_q().wait()
                for which in range(2):
                    load_own(which).wait()

            @pl.when(has_far)
            def _():
                attend(g, False)

            @pl.when(me < back)
            def _():
                attend(g, True)

            store_out(g).start()

    @pl.when(core == 0)
    def _():
        for which in range(2):
            send_core(which).wait_send()

    pltpu.make_async_copy(out_buf, out_hbm, out_sem).wait()
    for kind, condition in enumerate(
        (has_next, (odd_chip == 0) | has_far, (core == 1) & has_far, has_mid)
    ):

        @pl.when(condition)
        def _():
            for which in range(2):
                pltpu.make_async_remote_copy(
                    src_ref=own[which],
                    dst_ref=held[which].at[slot(1), :],
                    send_sem=send_sem.at[kind, which],
                    recv_sem=core_sem.at[1, which],
                    device_id=place(sibling),
                    device_id_type=MESH,
                ).wait_send()


def solution(mesh):
    n_head = mesh.shape["head"]
    count = mesh.shape["seq"] * n_head

    def on_device(queries, key_rows, value_rows):
        rows = queries.shape[0]
        assert rows * 4 == WINDOW and n_head % 4 == 0
        span = rows + WINDOW
        return pl.pallas_call(
            functools.partial(kernel, count, n_head),
            out_shape=jax.ShapeDtypeStruct(queries.shape, queries.dtype),
            in_specs=[pl.BlockSpec(memory_space=pl.ANY)] * 3,
            out_specs=pl.BlockSpec(memory_space=pl.ANY),
            scratch_shapes=[
                pltpu.VMEM(queries.shape, jnp.bfloat16),
                pltpu.VMEM((span, KV * HD), jnp.bfloat16),
                pltpu.VMEM((span, KV * HD), jnp.bfloat16),
                pltpu.VMEM(queries.shape, jnp.bfloat16),
                pltpu.SemaphoreType.DMA,
                pltpu.SemaphoreType.DMA((2,)),
                pltpu.SemaphoreType.DMA,
                pltpu.SemaphoreType.DMA((2, 2)),
                pltpu.SemaphoreType.DMA((4, 2)),
                pltpu.SemaphoreType.DMA((4, CHUNKS, 2)),
            ],
            compiler_params=pltpu.CompilerParams(
                collective_id=0, has_side_effects=True, vmem_limit_bytes=60 * 1024 * 1024
            ),
            cost_estimate=pl.CostEstimate(
                flops=4 * HQ * rows * span * HD,
                bytes_accessed=16 * 1024 * 1024,
                transcendentals=HQ * rows * span,
            ),
        )(queries, key_rows, value_rows)

    placed = P(("seq", "head"), None)
    return jax.shard_map(
        on_device, mesh=mesh, in_specs=(placed, placed, placed), out_specs=placed, check_vma=False
    )
```

```python
import functools
import math

import jax
import jax.numpy as jnp
from jax import lax
from jax.experimental import pallas as pl
from jax.experimental.pallas import tpu as pltpu
from jax.sharding import PartitionSpec as P

HQ = 32
KV = 16
HD = 128
WINDOW = 1024
GROUP = HQ // KV
CHUNKS = 16
AHEAD = 4

MESH = pl.DeviceIdType.MESH
exponent_scale = 168.0 ** (-0.5) * math.log2(math.e)
neg_fill = -1e30


def kernel(
    count,
    n_head,
    q_hbm,
    k_hbm,
    v_hbm,
    out_ref,
    q_buf,
    k_buf,
    v_buf,
    q_sem,
    own_sem,
    core_sem,
    send_sem,
    recv_sem,
):
    rows = q_hbm.shape[0]
    back = WINDOW // rows
    heads = KV // CHUNKS
    width = heads * HD
    me = lax.axis_index("seq") * n_head + lax.axis_index("head")
    core = lax.rem(me, 2)
    odd_chip = lax.rem(me // 2, 2)
    sibling = me + 1 - 2 * core
    across = me + 2 - 4 * odd_chip
    has_next = me + back < count
    has_far = me >= back
    has_mid = me >= 2

    def place(rank):
        return (rank // n_head, lax.rem(rank, n_head))

    def columns(g):
        return pl.ds(pl.multiple_of(g * width, width), width)

    def slot(distance):
        return pl.ds((back - distance) * rows, rows)

    own = (k_hbm, v_hbm)
    held = (k_buf, v_buf)

    def send(kind, g, which, source, distance, target):
        if source == 0:
            src = own[which].at[:, columns(g)]
        else:
            src = held[which].at[slot(source), columns(g)]
        return pltpu.make_async_remote_copy(
            src_ref=src,
            dst_ref=held[which].at[slot(distance), columns(g)],
            send_sem=send_sem.at[kind, which],
            recv_sem=recv_sem.at[distance - 1, g, which],
            device_id=place(target),
            device_id_type=MESH,
        )

    def sends(g):
        return {
            "next": (has_next, 0, 0, back, me + back),
            "up": (odd_chip == 0, 1, 0, 2, across),
            "down": ((odd_chip == 1) & has_far, 1, back, 2, across),
            "far": ((core == 1) & has_far, 2, back, 3, sibling),
            "mid0": ((core == 0) & has_mid, 3, 2, 3, sibling),
            "mid1": ((core == 1) & has_mid, 3, 2, 1, sibling),
        }

    def start(g, which, *names):
        for name in names:
            condition, kind, source, distance, target = sends(g)[name]

            @pl.when(condition)
            def _():
                send(kind, g, which, source, distance, target).start()

    def arrived(g, which, distance):
        send(0, g, which, distance, distance, sibling).wait_recv()

    def load_own(which):
        return pltpu.make_async_copy(own[which], held[which].at[slot(0), :], own_sem.at[which])

    def send_core(which):
        return pltpu.make_async_remote_copy(
            src_ref=own[which],
            dst_ref=held[which].at[slot(1), :],
            send_sem=core_sem.at[0, which],
            recv_sem=core_sem.at[1, which],
            device_id=place(sibling),
            device_id_type=MESH,
        )

    def q_columns(g):
        return pl.ds(pl.multiple_of(g * width * GROUP, width * GROUP), width * GROUP)

    def load_q():
        return pltpu.make_async_copy(q_hbm, q_buf, q_sem)

    def attend(g, checked):
        row = lax.broadcasted_iota(jnp.int32, (rows, rows), 0)
        column = lax.broadcasted_iota(jnp.int32, (rows, rows), 1)
        for local in range(heads):
            head = g * heads + local
            at = pl.ds(pl.multiple_of(head * HD, HD), HD)
            keys = k_buf[:, at]
            values = v_buf[:, at]
            for r in range(GROUP):
                q_at = pl.ds(pl.multiple_of((head * GROUP + r) * HD, HD), HD)
                scores = lax.dot_general(
                    q_buf[:, q_at], keys, (((1,), (1,)), ((), ())), preferred_element_type=jnp.float32
                )
                pieces = []
                for j in range(back + 1):
                    piece = scores[:, j * rows : (j + 1) * rows]
                    keep = None
                    if j == 0:
                        keep = column > row
                    elif j == back:
                        keep = column <= row
                    if checked and j < back:
                        there = jnp.full((rows, rows), me - back + j, jnp.int32) >= 0
                        keep = there if keep is None else keep & there
                    pieces.append(piece if keep is None else jnp.where(keep, piece, neg_fill))
                scores = jnp.concatenate(pieces, axis=1)
                peak = jnp.max(scores, axis=1, keepdims=True)
                expo = jnp.exp2((scores - peak) * exponent_scale)
                total = jnp.sum(expo, axis=1, keepdims=True)
                mixed = jnp.dot(expo.astype(jnp.bfloat16), values, preferred_element_type=jnp.float32)
                out_ref[:, q_at] = (mixed / total).astype(jnp.bfloat16)

    barrier = pltpu.get_barrier_semaphore()
    for target in (sibling, across):
        pl.semaphore_signal(barrier, inc=1, device_id=place(target), device_id_type=MESH)

    @pl.when(has_next)
    def _():
        pl.semaphore_signal(barrier, inc=1, device_id=place(me + back), device_id_type=MESH)

    @pl.when(has_far)
    def _():
        pl.semaphore_signal(barrier, inc=1, device_id=place(me - back), device_id_type=MESH)

    pl.semaphore_wait(barrier, 2 + has_next.astype(jnp.int32) + has_far.astype(jnp.int32))

    def start_own(g):
        for which in range(2):
            start(g, which, "next", "up")

    for g in range(AHEAD):
        start_own(g)

    @pl.when(core == 0)
    def _():
        for which in range(2):
            send_core(which).start()

    load_q().start()
    for which in range(2):
        load_own(which).start()

    for distance in range(1, back + 1):

        @pl.when(me < distance)
        def _():
            for which in range(2):
                held[which][slot(distance), :] = jnp.zeros((rows, KV * HD), jnp.bfloat16)

    @pl.loop(0, CHUNKS + 2)
    def _(t):
        @pl.when(t + AHEAD < CHUNKS)
        def _():
            start_own(t + AHEAD)

        @pl.when((t < CHUNKS) & has_far)
        def _():
            for which in range(2):
                arrived(t, which, back)
                start(t, which, "down", "far")

        mid = t - 1

        @pl.when((mid >= 0) & (mid < CHUNKS) & has_mid)
        def _():
            for which in range(2):
                arrived(mid, which, 2)
                start(mid, which, "mid0", "mid1")

        g = t - 2

        @pl.when(g >= 0)
        def _():
            @pl.when((core == 0) & (me >= 1))
            def _():
                for which in range(2):
                    arrived(g, which, 1)

            @pl.when((core == 1) & (g == 0))
            def _():
                for which in range(2):
                    send_core(which).wait_recv()

            @pl.when(me >= 3)
            def _():
                for which in range(2):
                    arrived(g, which, 3)

            @pl.when(g == 0)
            def _():
                load_q().wait()
                for which in range(2):
                    load_own(which).wait()

            @pl.when(has_far)
            def _():
                attend(g, False)

            @pl.when(me < back)
            def _():
                attend(g, True)

    @pl.when(core == 0)
    def _():
        for which in range(2):
            send_core(which).wait_send()

    for kind, condition in enumerate(
        (has_next, (odd_chip == 0) | has_far, (core == 1) & has_far, has_mid)
    ):

        @pl.when(condition)
        def _():
            for which in range(2):
                pltpu.make_async_remote_copy(
                    src_ref=own[which],
                    dst_ref=held[which].at[slot(1), :],
                    send_sem=send_sem.at[kind, which],
                    recv_sem=core_sem.at[1, which],
                    device_id=place(sibling),
                    device_id_type=MESH,
                ).wait_send()


def solution(mesh):
    n_head = mesh.shape["head"]
    count = mesh.shape["seq"] * n_head

    def on_device(queries, key_rows, value_rows):
        rows = queries.shape[0]
        assert rows * 4 == WINDOW and n_head % 4 == 0
        span = rows + WINDOW
        return pl.pallas_call(
            functools.partial(kernel, count, n_head),
            out_shape=pltpu.VMEM(queries.shape, queries.dtype),
            in_specs=[pl.BlockSpec(memory_space=pl.ANY)] * 3,
            out_specs=pl.BlockSpec(memory_space=pltpu.VMEM),
            scratch_shapes=[
                pltpu.VMEM(queries.shape, jnp.bfloat16),
                pltpu.VMEM((span, KV * HD), jnp.bfloat16),
                pltpu.VMEM((span, KV * HD), jnp.bfloat16),
                pltpu.SemaphoreType.DMA,
                pltpu.SemaphoreType.DMA((2,)),
                pltpu.SemaphoreType.DMA((2, 2)),
                pltpu.SemaphoreType.DMA((4, 2)),
                pltpu.SemaphoreType.DMA((4, CHUNKS, 2)),
            ],
            compiler_params=pltpu.CompilerParams(
                collective_id=0, has_side_effects=True, vmem_limit_bytes=48 * 1024 * 1024
            ),
            cost_estimate=pl.CostEstimate(
                flops=4 * HQ * rows * span * HD,
                bytes_accessed=16 * 1024 * 1024,
                transcendentals=HQ * rows * span,
            ),
        )(*(pltpu.with_memory_space_constraint(x, pltpu.HBM) for x in (queries, key_rows, value_rows)))

    placed = P(("seq", "head"), None)
    return jax.shard_map(
        on_device, mesh=mesh, in_specs=(placed, placed, placed), out_specs=placed, check_vma=False
    )
```
